1024 devices in a mesh: outer: 64 (over z, y_lo), blk: 16 (over y_hi, x, core).
Axes of the slice: x: 4, y: 4 (y_hi: 2, y_lo: 2; y = y_hi * 2 + y_lo), z: 32, core: 2. Of those that a mesh axis runs over, the one named last changes fastest.
Arguments:
- picture_embeds: bfloat16 [262144, 1152], P(('outer', 'blk')), may hold values from -0.1875 to 0.1875
- caption_embeds: bfloat16 [262144, 1152], P(('outer', 'blk')), may hold values from -0.1875 to 0.1875
- sharpness_factor: float32 [1], replicated, may hold values from 60 to 120
- offset_term: float32 [1], replicated, may hold values from -4 to -2
Outputs:
- image_grad: float32 [262144, 1152], P(('outer', 'blk'))
- caption_derivative: float32 [262144, 1152], P(('outer', 'blk'))
The draws below stay inside these ranges and needn't reach their ends.
All inputs are finite; a program needn't handle non-finite values.
Results may differ from the reference program's by a relative error of at most 0.007.
Values may be sent and summed in bfloat16 or wider, within the bound.
No kernel may reach another device: no remote copies, remote signals or barrier semaphores. Data moves between devices by JAX's collectives and lax.ppermute only.
A program may use at most 32 MiB of HBM per device.

```python
import math
import jax
import jax.numpy as jnp
from jax import lax

D = 1152
ROWS = 256
HALF = 2
TOKENS = 262144
DEVICES = 1024


def steps_of(own_key, extent, cuts, low, high):
    factor_of = 1.0
    for position, shards_of in cuts:
        steps = jax.random.uniform(jax.random.fold_in(jax.random.fold_in(own_key, 6), position), (shards_of,), jnp.float32, low / len(cuts), high / len(cuts))
        factor_of = factor_of * jnp.repeat(jnp.exp(steps), extent[position] // shards_of).reshape((-1,) + (1,) * (len(extent) - 1 - position))
    return factor_of


def normal_values(stream_key, shape, spread, reach, pieces=(), kind=jnp.bfloat16):
    loudness = steps_of(stream_key, shape, pieces, -0.22, 0.18) if pieces else 1.0
    drawn = jax.random.normal(stream_key, shape, jnp.float32) * spread * loudness
    return jnp.minimum(jnp.maximum(drawn, -reach), reach).astype(kind)


def setup_inputs(seed: int = 0) -> dict:
    keys = jax.random.split(jax.random.key(seed), 5)
    return {
        "picture_embeds": normal_values(keys[0], (TOKENS, D), D ** -0.5, 0.1875, ((0, 1024),)),
        "caption_embeds": normal_values(keys[1], (TOKENS, D), D ** -0.5, 0.1875, ((0, 1024),)),
        "sharpness_factor": jnp.clip(jnp.exp(jax.random.uniform(keys[2], (1,), jnp.float32, math.log(60.0), math.log(120.0))), 60.0, 120.0),
        "offset_term": jnp.clip(jax.random.uniform(keys[3], (1,), jnp.float32, -4.0, -2.0), -4.0, -2.0),
    }


def unit_rows(quantities_array):
    wide = quantities_array.astype(jnp.float32)
    norm = jnp.sqrt(lax.optimization_barrier(jnp.sum(wide * wide, axis=-1, keepdims=True)) + 1e-06)
    return (wide / norm, norm)

def reference(picture_embeds, caption_embeds, sharpness_factor, offset_term):
    image_unit_vectors, norm_x = unit_rows(picture_embeds.reshape(DEVICES, ROWS, D))
    unit_y, norm_y = unit_rows(caption_embeds.reshape(DEVICES, ROWS, D))
    image_normalized = image_unit_vectors.astype(jnp.bfloat16).astype(jnp.float32)
    text_n = unit_y.astype(jnp.bfloat16).astype(jnp.float32)
    inverse_warmth = sharpness_factor[0]
    offset = offset_term[0]
    span = 2 * HALF + 1
    eye = jnp.eye(ROWS, dtype=jnp.float32)
    derivative_input = jnp.zeros((DEVICES, ROWS, D), jnp.float32)
    text_unit_gradient = jnp.zeros((DEVICES, ROWS, D), jnp.float32)
    high = lax.Precision.HIGHEST
    for step in range(-HALF, HALF + 1):
        block = jnp.roll(text_n, -step, axis=0)
        pair_scores = inverse_warmth * jnp.einsum('gid,gjd->gij', image_normalized, block, precision=high) + offset
        if step == 0:
            label = 2.0 * eye - 1.0
        else:
            label = -jnp.ones((ROWS, ROWS), jnp.float32)
        grad_z = (-label * jax.nn.sigmoid(-label * pair_scores) / span).astype(jnp.bfloat16).astype(jnp.float32)
        derivative_input = derivative_input + inverse_warmth * jnp.einsum('gij,gjd->gid', grad_z, block, precision=high)
        part = (inverse_warmth * jnp.einsum('gij,gid->gjd', grad_z, image_normalized, precision=high)).astype(jnp.bfloat16)
        text_unit_gradient = text_unit_gradient + jnp.roll(part, step, axis=0).astype(jnp.float32)
    image_grad = (derivative_input - image_unit_vectors * lax.optimization_barrier(jnp.sum(image_unit_vectors * derivative_input, axis=-1, keepdims=True))) / norm_x
    caption_derivative = (text_unit_gradient - unit_y * lax.optimization_barrier(jnp.sum(unit_y * text_unit_gradient, axis=-1, keepdims=True))) / norm_y
    return (image_grad.reshape(TOKENS, D), caption_derivative.reshape(TOKENS, D))
```

```python
import jax
import jax.numpy as jnp
from jax import lax
from jax.experimental import pallas as pl
from jax.experimental.pallas import tpu as pltpu
from jax.sharding import PartitionSpec as P

HALF = 2
SPAN = 2 * HALF + 1
AXES = ("outer", "blk")
MIB = 1024 * 1024


def unit_rows(block):
    wide = block.astype(jnp.float32)
    norm = jnp.sqrt(jnp.sum(wide * wide, axis=-1, keepdims=True) + 1e-06)
    inverse = 1.0 / norm
    return wide * inverse, inverse


def dot_nt(a, b):
    return lax.dot_general(a, b, (((1,), (1,)), ((), ())), preferred_element_type=jnp.float32)


def dot_tn(a, b):
    return lax.dot_general(a, b, (((0,), (0,)), ((), ())), preferred_element_type=jnp.float32)


def own_kernel(scale, offset, x, y, x_n, y_n, grad_x, grad_y):
    x_n[...] = unit_rows(x[...])[0].astype(jnp.bfloat16)
    y_n[...] = unit_rows(y[...])[0].astype(jnp.bfloat16)
    z = scale[0] * dot_nt(x_n[...], y_n[...]) + offset[0]
    rows = lax.broadcasted_iota(jnp.int32, z.shape, 0)
    cols = lax.broadcasted_iota(jnp.int32, z.shape, 1)
    label = jnp.where(rows == cols, 1.0, -1.0).astype(jnp.float32)
    grad_z = (-label * jax.nn.sigmoid(-label * z) / SPAN).astype(jnp.bfloat16)
    grad_x[...] = jnp.dot(grad_z, y_n[...], preferred_element_type=jnp.float32)
    grad_y[...] = dot_tn(grad_z, x_n[...])


def met(scale, offset, own_n, other):
    other_n = unit_rows(other[...])[0].astype(jnp.bfloat16)
    z = scale[0] * dot_nt(own_n[...], other_n) + offset[0]
    grad_z = (jax.nn.sigmoid(z) / SPAN).astype(jnp.bfloat16)
    return jnp.dot(grad_z, other_n, preferred_element_type=jnp.float32)


def add_kernel(scale, offset, own_n, total, *others_and_out):
    *others, out = others_and_out
    out[...] = total[...] + met(scale, offset, own_n, others[0])
    for other in others[1:]:
        out[...] += met(scale, offset, own_n, other)


def end_kernel(scale, offset, own, own_n, total, *others_and_out):
    *others, out = others_and_out
    add_kernel(scale, offset, own_n, total, *others, out)
    unit, inverse = unit_rows(own[...])
    grad = scale[0] * out[...]
    out[...] = (grad - unit * jnp.sum(unit * grad, axis=-1, keepdims=True)) * inverse


def call(kernel, outs, scalars, arrays, matmuls):
    rows, width = arrays[0].shape
    whole = pl.BlockSpec(memory_space=pltpu.VMEM)
    single = pl.BlockSpec(memory_space=pltpu.SMEM)
    shapes = [jax.ShapeDtypeStruct((rows, width), t) for t in outs]
    moved = sum(a.size * a.dtype.itemsize for a in arrays) + sum(rows * width * jnp.dtype(t).itemsize for t in outs)
    return pl.pallas_call(
        kernel,
        out_shape=shapes,
        in_specs=[single] * len(scalars) + [whole] * len(arrays),
        out_specs=[whole] * len(outs),
        compiler_params=pltpu.CompilerParams(vmem_limit_bytes=16 * MIB),
        cost_estimate=pl.CostEstimate(
            flops=matmuls * 2 * rows * rows * width, bytes_accessed=moved, transcendentals=matmuls * rows * rows // 2
        ),
    )(*scalars, *arrays)


def per_device(picture_embeds, caption_embeds, sharpness_factor, offset_term):
    scalars = (sharpness_factor, offset_term)
    n = lax.axis_size(AXES)
    near = [(g, (g + 2) % n if g % 2 else (g - 2) % n) for g in range(n)]
    far = [(g, (g - 2) % n if g % 2 else (g + 2) % n) for g in range(n)]
    swap = [(g, g ^ 1) for g in range(n)]

    def sent(v, perm):
        return lax.ppermute(v, AXES, perm)

    f32, bf16 = jnp.float32, jnp.bfloat16
    x_n, y_n, grad_x, grad_y = call(own_kernel, (bf16, bf16, f32, f32), scalars, (picture_embeds, caption_embeds), 3)
    results = []
    for own, own_n, total, other in (
        (picture_embeds, x_n, grad_x, caption_embeds),
        (caption_embeds, y_n, grad_y, picture_embeds),
    ):
        shared = sent(other, near)
        mate = sent(other, swap)
        last = sent(other, far)
        relayed = sent(shared, swap)
        (total,) = call(add_kernel, (f32,), scalars, (own_n, total, mate), 2)
        (total,) = call(add_kernel, (f32,), scalars, (own_n, total, shared), 2)
        (out,) = call(end_kernel, (f32,), scalars, (own, own_n, total, last, relayed), 4)
        results.append(out)
    return tuple(results)


def solution(mesh):
    return jax.shard_map(
        per_device,
        mesh=mesh,
        in_specs=(P(AXES, None), P(AXES, None), P(), P()),
        out_specs=(P(AXES, None), P(AXES, None)),
        check_vma=False,
    )
```

```python
import functools

import jax
import jax.numpy as jnp
from jax import lax
from jax.experimental import pallas as pl
from jax.experimental.pallas import tpu as pltpu
from jax.sharding import PartitionSpec as P

HALF = 2
SPAN = 2 * HALF + 1
AXES = ("outer", "blk")
MIB = 1024 * 1024
CHUNKS = 4
F32, BF16 = jnp.float32, jnp.bfloat16


def inverse_norm(wide):
    return 1.0 / jnp.sqrt(jnp.sum(wide * wide, axis=-1, keepdims=True) + 1e-06)


def normalized(block):
    wide = block.astype(F32)
    return (wide * inverse_norm(wide)).astype(BF16)


def dot(a, b):
    return jnp.dot(a, b, preferred_element_type=F32)


def logits(scale, offset, own_n, other_n):
    z = lax.dot_general(own_n, other_n, (((1,), (1,)), ((), ())), preferred_element_type=F32)
    return scale[0] * z + offset[0]


def pair_grad(scale, offset, own_n, other_n):
    return (jax.nn.sigmoid(logits(scale, offset, own_n, other_n)) / SPAN).astype(BF16)


def halves(ref):
    rows = ref.shape[0] // 2
    return ref[:rows], ref[rows:]


def prepare_kernel(x, y, raw, pair, inverse, sem):
    rows = x.shape[0]
    step = rows // CHUNKS
    copies = []
    for side, source in enumerate((x, y)):
        for c in range(CHUNKS):
            copies.append(
                pltpu.make_async_copy(
                    source.at[pl.ds(c * step, step)],
                    raw.at[pl.ds(side * rows + c * step, step)],
                    sem.at[side * CHUNKS + c],
                )
            )
    for copy in copies:
        copy.start()
    for c, copy in enumerate(copies):
        copy.wait()
        part = slice(c * step, (c + 1) * step)
        wide = raw[part].astype(F32)
        inv = inverse_norm(wide)
        inverse[part] = inv
        pair[part] = (wide * inv).astype(BF16)


def own_kernel(scale, offset, pair, sum_x, sum_y):
    x_n, y_n = halves(pair)
    z = logits(scale, offset, x_n, y_n)
    rows = lax.broadcasted_iota(jnp.int32, z.shape, 0)
    cols = lax.broadcasted_iota(jnp.int32, z.shape, 1)
    label = jnp.where(rows == cols, 1.0, -1.0).astype(F32)
    grad_z = (-label * jax.nn.sigmoid(-label * z) / SPAN).astype(BF16)
    sum_x[...] = dot(grad_z, y_n)
    sum_y[...] = lax.dot_general(grad_z, x_n, (((0,), (0,)), ((), ())), preferred_element_type=F32)


def both_kernel(scale, offset, pair, total_x, total_y, other, sum_x, sum_y):
    x_n, y_n = halves(pair)
    other_x, other_y = halves(other)
    grad_x = pair_grad(scale, offset, x_n, other_y)
    grad_y = pair_grad(scale, offset, y_n, other_x)
    sum_x[...] = total_x[...] + dot(grad_x, other_y)
    sum_y[...] = total_y[...] + dot(grad_y, other_x)


def one_kernel(side, scale, offset, pair, total, other, out):
    own_n = halves(pair)[side]
    other_n = normalized(other[...])
    out[...] = total[...] + dot(pair_grad(scale, offset, own_n, other_n), other_n)


def end_kernel(side, scale, offset, rim, pair, raw, inverse, total, relayed, late, late_relayed, out, full, sem):
    own_n = halves(pair)[side]
    other_n = normalized(relayed[...])
    full[...] = total[...] + dot(pair_grad(scale, offset, own_n, other_n), other_n)

    @pl.when(rim[0] == 1)
    def _():
        for ref in (late, late_relayed):
            other_n = halves(ref)[1 - side]
            full[...] += dot(pair_grad(scale, offset, own_n, other_n), other_n)

    rows = full.shape[0]
    step = rows // CHUNKS
    copies = []
    for c in range(CHUNKS):
        part = slice(c * step, (c + 1) * step)
        mine = slice(side * rows + c * step, side * rows + (c + 1) * step)
        inv = inverse[mine]
        wide = raw[mine].astype(F32)
        grad = scale[0] * full[part]
        along = inv * inv * jnp.sum(wide * grad, axis=-1, keepdims=True)
        full[part] = (grad - wide * along) * inv
        copy = pltpu.make_async_copy(full.at[pl.ds(c * step, step)], out.at[pl.ds(c * step, step)], sem.at[c])
        copy.start()
        copies.append(copy)
    for copy in copies:
        copy.wait()


VMEM = pl.BlockSpec(memory_space=pltpu.VMEM)
SMEM = pl.BlockSpec(memory_space=pltpu.SMEM)
ANY = pl.BlockSpec(memory_space=pl.ANY)


def call(kernel, outs, arrays, small=0, in_spec=VMEM, out_spec=VMEM, scratch=()):
    return pl.pallas_call(
        kernel,
        out_shape=[jax.ShapeDtypeStruct(*o) for o in outs],
        in_specs=[SMEM] * small + [in_spec] * (len(arrays) - small),
        out_specs=[out_spec] * len(outs),
        scratch_shapes=list(scratch),
        compiler_params=pltpu.CompilerParams(vmem_limit_bytes=16 * MIB),
        cost_estimate=pl.CostEstimate(flops=1, bytes_accessed=1, transcendentals=0),
    )(*arrays)


def after(value, *events):
    return lax.optimization_barrier((value, *events))[0]


def per_device(picture_embeds, caption_embeds, sharpness_factor, offset_term):
    scalars = (sharpness_factor, offset_term)
    n = lax.axis_size(AXES)
    rows, width = picture_embeds.shape
    one, two = (rows, width), (2 * rows, width)
    here = lax.axis_index(AXES)
    rim = ((here == 0) | (here >= n - 2)).astype(jnp.int32).reshape(1)

    near = [(g, (g + 2) % n if g % 2 else (g - 2) % n) for g in range(n) if g != 0]
    far = [(g, (g - 2) % n if g % 2 else (g + 2) % n) for g in range(n) if g != n - 2]
    swap = [(g, g ^ 1) for g in range(n)]
    closing = [(0, n - 2), (n - 2, 0)]
    closing_relay = [(n - 2, n - 1)]

    def sent(value, perm):
        return lax.ppermute(value, AXES, perm)

    near_text = sent(caption_embeds, near)
    raw, pair, inverse = call(
        prepare_kernel,
        [(two, BF16), (two, BF16), ((2 * rows, 1), F32)],
        (picture_embeds, caption_embeds),
        in_spec=ANY,
        scratch=[pltpu.SemaphoreType.DMA((2 * CHUNKS,))],
    )
    far_pair = sent(pair, far)
    near_image = sent(after(picture_embeds, pair), near)
    sum_x, sum_y = call(own_kernel, [(one, F32)] * 2, (*scalars, pair), small=2)
    mate_pair = sent(after(pair, sum_x, sum_y), swap)
    relayed_text = sent(near_text, swap)
    (sum_x,) = call(functools.partial(one_kernel, 0), [(one, F32)], (*scalars, pair, sum_x, near_text), small=2)
    late_pair = sent(after(pair, sum_x), closing)
    relayed_image = sent(after(near_image, relayed_text, sum_x), swap)
    (sum_y,) = call(functools.partial(one_kernel, 1), [(one, F32)], (*scalars, pair, sum_y, near_image), small=2)
    sum_x, sum_y = call(both_kernel, [(one, F32)] * 2, (*scalars, pair, sum_x, sum_y, far_pair), small=2)
    sum_x, sum_y = call(both_kernel, [(one, F32)] * 2, (*scalars, pair, sum_x, sum_y, mate_pair), small=2)
    late_relayed = sent(after(late_pair, relayed_text, relayed_image, sum_x, sum_y), closing_relay)
    sums = (sum_x, sum_y)
    return tuple(
        call(
            functools.partial(end_kernel, side),
            [(one, F32)],
            (*scalars, rim, pair, raw, inverse, sums[side], relayed, late_pair, late_relayed),
            small=3,
            out_spec=ANY,
            scratch=[pltpu.VMEM(one, F32), pltpu.SemaphoreType.DMA((CHUNKS,))],
        )[0]
        for side, relayed in enumerate((relayed_text, relayed_image))
    )


def solution(mesh):
    return jax.shard_map(
        per_device,
        mesh=mesh,
        in_specs=(P(AXES, None), P(AXES, None), P(), P()),
        out_specs=(P(AXES, None), P(AXES, None)),
        check_vma=False,
    )
```

```python
import jax
import jax.numpy as jnp
from jax import lax
from jax.experimental import pallas as pl
from jax.experimental.pallas import tpu as pltpu
from jax.sharding import PartitionSpec as P

HALF = 2
SPAN = 2 * HALF + 1
AXES = ("outer", "blk")
MIB = 1024 * 1024
CHUNKS = 4
F32, BF16 = jnp.float32, jnp.bfloat16


def inverse_norm(wide):
    return 1.0 / jnp.sqrt(jnp.sum(wide * wide, axis=-1, keepdims=True) + 1e-06)


def normalized(block):
    wide = block.astype(F32)
    return (wide * inverse_norm(wide)).astype(BF16)


def dot(a, b):
    return jnp.dot(a, b, preferred_element_type=F32)


def logits(scale, offset, own_n, other_n):
    z = lax.dot_general(own_n, other_n, (((1,), (1,)), ((), ())), preferred_element_type=F32)
    return scale[0] * z + offset[0]


def pair_grad(scale, offset, own_n, other_n):
    return (jax.nn.sigmoid(logits(scale, offset, own_n, other_n)) / SPAN).astype(BF16)


def halves(ref):
    rows = ref.shape[0] // 2
    return ref[:rows], ref[rows:]


def side_grads(scale, offset, mine, theirs):
    return [pair_grad(scale, offset, own_n, other_n) for own_n, other_n in zip(mine, theirs[::-1])]


def prepare_kernel(x, y, pair, raw, sem):
    rows = x.shape[0]
    step = rows // CHUNKS
    copies = []
    for side, source in enumerate((x, y)):
        for c in range(CHUNKS):
            copies.append(
                pltpu.make_async_copy(
                    source.at[pl.ds(c * step, step)],
                    raw.at[pl.ds(side * rows + c * step, step)],
                    sem.at[side * CHUNKS + c],
                )
            )
    for copy in copies:
        copy.start()
    for c, copy in enumerate(copies):
        copy.wait()
        part = slice(c * step, (c + 1) * step)
        wide = raw[part].astype(F32)
        pair[part] = (wide * inverse_norm(wide)).astype(BF16)


def early_kernel(rim, scale, offset, pair, mate, picked, own_grad, mate_grad_x, mate_grad_y):
    @pl.when(rim[0] == 1)
    def _():
        picked[...] = mate[...]

    @pl.when(rim[0] != 1)
    def _():
        picked[...] = pair[...]

    mine = halves(pair)
    z = logits(scale, offset, *mine)
    rows = lax.broadcasted_iota(jnp.int32, z.shape, 0)
    cols = lax.broadcasted_iota(jnp.int32, z.shape, 1)
    label = jnp.where(rows == cols, 1.0, -1.0).astype(F32)
    own_grad[...] = (-label * jax.nn.sigmoid(-label * z) / SPAN).astype(BF16)
    mate_grad_x[...], mate_grad_y[...] = side_grads(scale, offset, mine, halves(mate))


def middle_kernel(
    scale, offset, pair, mate, own_grad, mate_grad_x, mate_grad_y, near_x, near_y,
    sum_x, sum_y, held_x, held_y, sem,
):
    copies = [
        pltpu.make_async_copy(source, held, sem.at[k])
        for k, (source, held) in enumerate(((near_y, held_y), (near_x, held_x)))
    ]
    for copy in copies:
        copy.start()
    mine, mates = halves(pair), halves(mate)
    sum_x[...] = dot(own_grad[...], mine[1]) + dot(mate_grad_x[...], mates[1])
    sum_y[...] = (
        lax.dot_general(own_grad[...], mine[0], (((0,), (0,)), ((), ())), preferred_element_type=F32)
        + dot(mate_grad_y[...], mates[0])
    )
    for copy in copies:
        copy.wait()
    nears = normalized(held_x[...]), normalized(held_y[...])
    grad_x, grad_y = side_grads(scale, offset, mine, nears)
    sum_x[...] += dot(grad_x, nears[1])
    sum_y[...] += dot(grad_y, nears[0])


def end_kernel(
    rim, scale, offset, pair, total_x, total_y, far, relay_x, relay_y, x, y, late,
    out_x, out_y, full, raw, spare, raw_sem, spare_sem, sem,
):
    rows = total_x.shape[0]
    step = rows // CHUNKS
    loads = [
        pltpu.make_async_copy(source, raw.at[pl.ds(side * rows, rows)], raw_sem.at[side])
        for side, source in enumerate((x, y))
    ]
    for load in loads:
        load.start()
    mine, fars = halves(pair), halves(far)
    relays = normalized(relay_x[...]), normalized(relay_y[...])
    far_grads = side_grads(scale, offset, mine, fars)
    relay_grads = side_grads(scale, offset, mine, relays)
    for side, total in enumerate((total_x, total_y)):
        full[side * rows : (side + 1) * rows] = (
            total[...] + dot(far_grads[side], fars[1 - side]) + dot(relay_grads[side], relays[1 - side])
        )

    @pl.when(rim[0] > 0)
    def _():
        copy = pltpu.make_async_copy(late, spare, spare_sem)
        copy.start()
        copy.wait()
        lates = halves(spare)
        late_grads = side_grads(scale, offset, mine, lates)
        for side in range(2):
            full[side * rows : (side + 1) * rows] += dot(late_grads[side], lates[1 - side])

    copies = []
    for side, out in enumerate((out_x, out_y)):
        loads[side].wait()
        for c in range(CHUNKS):
            part = slice(side * rows + c * step, side * rows + (c + 1) * step)
            wide = raw[part].astype(F32)
            inv = inverse_norm(wide)
            grad = scale[0] * full[part]
            along = inv * inv * jnp.sum(wide * grad, axis=-1, keepdims=True)
            full[part] = (grad - wide * along) * inv
            copy = pltpu.make_async_copy(
                full.at[pl.ds(side * rows + c * step, step)],
                out.at[pl.ds(c * step, step)],
                sem.at[side * CHUNKS + c],
            )
            copy.start()
            copies.append(copy)
    for copy in copies:
        copy.wait()


VMEM = pl.BlockSpec(memory_space=pltpu.VMEM)
SMEM = pl.BlockSpec(memory_space=pltpu.SMEM)
ANY = pl.BlockSpec(memory_space=pl.ANY)


def call(kernel, outs, arrays, small=0, loose=0, in_spec=VMEM, out_spec=VMEM, scratch=()):
    return pl.pallas_call(
        kernel,
        out_shape=[jax.ShapeDtypeStruct(*o) for o in outs],
        in_specs=[SMEM] * small + [in_spec] * (len(arrays) - small - loose) + [ANY] * loose,
        out_specs=[out_spec] * len(outs),
        scratch_shapes=list(scratch),
        compiler_params=pltpu.CompilerParams(vmem_limit_bytes=12 * MIB),
        cost_estimate=pl.CostEstimate(flops=1, bytes_accessed=1, transcendentals=0),
    )(*arrays)


def after(value, *events):
    return lax.optimization_barrier((value, *events))[0]


def per_device(picture_embeds, caption_embeds, sharpness_factor, offset_term):
    scalars = (sharpness_factor, offset_term)
    n = lax.axis_size(AXES)
    rows, width = picture_embeds.shape
    one, two, square = (rows, width), (2 * rows, width), (rows, rows)
    here = lax.axis_index(AXES)
    rim = jnp.where(here == 0, 1, jnp.where(here == n - 1, 2, 0)).astype(jnp.int32).reshape(1)

    near = [(g, (g + 2) % n if g % 2 else (g - 2) % n) for g in range(n)]
    far = [(g, (g - 2) % n if g % 2 else (g + 2) % n) for g in range(n) if g not in (1, n - 2)]
    swap = [(g, g ^ 1) for g in range(n)]
    closing = [(0, n - 1), (n - 2, 0)]

    def sent(value, perm):
        return lax.ppermute(value, AXES, perm)

    near_y = sent(caption_embeds, near)
    near_x = sent(picture_embeds, near)
    (pair,) = call(
        prepare_kernel,
        [(two, BF16)],
        (picture_embeds, caption_embeds),
        in_spec=ANY,
        scratch=[pltpu.VMEM(two, BF16), pltpu.SemaphoreType.DMA((2 * CHUNKS,))],
    )
    far_pair = sent(pair, far)
    mate_pair = sent(pair, swap)
    picked, *grads = call(
        early_kernel, [(two, BF16)] + [(square, BF16)] * 3, (rim, *scalars, pair, mate_pair), small=3
    )
    late_pair = sent(picked, closing)
    relay_y = sent(after(near_y, *grads), swap)
    relay_x = sent(after(near_x, *grads), swap)
    sums = call(
        middle_kernel,
        [(one, F32)] * 2,
        (*scalars, pair, mate_pair, *grads, near_x, near_y),
        small=2,
        loose=2,
        scratch=[pltpu.VMEM(one, BF16), pltpu.VMEM(one, BF16), pltpu.SemaphoreType.DMA((2,))],
    )
    return call(
        end_kernel,
        [(one, F32)] * 2,
        (rim, *scalars, pair, *sums, far_pair, relay_x, relay_y, picture_embeds, caption_embeds, late_pair),
        small=3,
        loose=3,
        out_spec=ANY,
        scratch=[
            pltpu.VMEM(two, F32),
            pltpu.VMEM(two, BF16),
            pltpu.VMEM(two, BF16),
            pltpu.SemaphoreType.DMA((2,)),
            pltpu.SemaphoreType.DMA(()),
            pltpu.SemaphoreType.DMA((2 * CHUNKS,)),
        ],
    )


def solution(mesh):
    return jax.shard_map(
        per_device,
        mesh=mesh,
        in_specs=(P(AXES, None), P(AXES, None), P(), P()),
        out_specs=(P(AXES, None), P(AXES, None)),
        check_vma=False,
    )
```

```python
import jax
import jax.numpy as jnp
from jax import lax
from jax.experimental import pallas as pl
from jax.experimental.pallas import tpu as pltpu
from jax.sharding import PartitionSpec as P

HALF = 2
SPAN = 2 * HALF + 1
AXES = ("outer", "blk")
MIB = 1024 * 1024
CHUNKS = 4
F32, BF16 = jnp.float32, jnp.bfloat16


def inverse_norm(wide):
    return 1.0 / jnp.sqrt(jnp.sum(wide * wide, axis=-1, keepdims=True) + 1e-06)


def normalized(block):
    wide = block.astype(F32)
    return (wide * inverse_norm(wide)).astype(BF16)


def dot(a, b):
    return jnp.dot(a, b, preferred_element_type=F32)


def logits(scale, offset, own_n, other_n):
    z = lax.dot_general(own_n, other_n, (((1,), (1,)), ((), ())), preferred_element_type=F32)
    return scale[0] * z + offset[0]


def pair_grad(scale, offset, own_n, other_n):
    return (jax.nn.sigmoid(logits(scale, offset, own_n, other_n)) / SPAN).astype(BF16)


def halves(ref):
    rows = ref.shape[0] // 2
    return ref[:rows], ref[rows:]


def side_grads(scale, offset, mine, theirs):
    return [pair_grad(scale, offset, own_n, other_n) for own_n, other_n in zip(mine, theirs[::-1])]


def prepare_kernel(x, y, pair, raw, sem):
    rows = x.shape[0]
    step = rows // CHUNKS
    copies = []
    for side, source in enumerate((x, y)):
        for c in range(CHUNKS):
            copies.append(
                pltpu.make_async_copy(
                    source.at[pl.ds(c * step, step)],
                    raw.at[pl.ds(side * rows + c * step, step)],
                    sem.at[side * CHUNKS + c],
                )
            )
    for copy in copies:
        copy.start()
    for c, copy in enumerate(copies):
        copy.wait()
        part = slice(c * step, (c + 1) * step)
        wide = raw[part].astype(F32)
        pair[part] = (wide * inverse_norm(wide)).astype(BF16)


def early_kernel(rim, scale, offset, pair, mate, picked, own_grad, mate_grad_x, mate_grad_y):
    @pl.when(rim[0] == 1)
    def _():
        picked[...] = mate[...]

    @pl.when(rim[0] != 1)
    def _():
        picked[...] = pair[...]

    mine = halves(pair)
    z = logits(scale, offset, *mine)
    rows = lax.broadcasted_iota(jnp.int32, z.shape, 0)
    cols = lax.broadcasted_iota(jnp.int32, z.shape, 1)
    label = jnp.where(rows == cols, 1.0, -1.0).astype(F32)
    own_grad[...] = (-label * jax.nn.sigmoid(-label * z) / SPAN).astype(BF16)
    mate_grad_x[...], mate_grad_y[...] = side_grads(scale, offset, mine, halves(mate))


def middle_kernel(
    scale, offset, pair, mate, own_grad, mate_grad_x, mate_grad_y, near_x, near_y,
    sum_x, sum_y, held_x, held_y, sem,
):
    copies = [
        pltpu.make_async_copy(source, held, sem.at[k])
        for k, (source, held) in enumerate(((near_y, held_y), (near_x, held_x)))
    ]
    for copy in copies:
        copy.start()
    mine, mates = halves(pair), halves(mate)
    sum_x[...] = dot(own_grad[...], mine[1]) + dot(mate_grad_x[...], mates[1])
    sum_y[...] = lax.dot_general(
        own_grad[...], mine[0], (((0,), (0,)), ((), ())), preferred_element_type=F32
    ) + dot(mate_grad_y[...], mates[0])
    for copy, held, own_n, out in zip(copies, (held_y, held_x), mine, (sum_x, sum_y)):
        copy.wait()
        other_n = normalized(held[...])
        out[...] += dot(pair_grad(scale, offset, own_n, other_n), other_n)


def end_kernel(
    rim, scale, offset, pair, total_x, total_y, far, relay_x, relay_y, x, y, late,
    out_x, out_y, full, raw, spare, raw_sem, spare_sem, sem,
):
    rows = total_x.shape[0]
    step = rows // CHUNKS
    loads = [
        pltpu.make_async_copy(source, raw.at[pl.ds(side * rows, rows)], raw_sem.at[side])
        for side, source in enumerate((x, y))
    ]
    for load in loads:
        load.start()
    mine, fars = halves(pair), halves(far)
    relays = normalized(relay_x[...]), normalized(relay_y[...])
    far_grads = side_grads(scale, offset, mine, fars)
    relay_grads = side_grads(scale, offset, mine, relays)
    for side, total in enumerate((total_x, total_y)):
        full[side * rows : (side + 1) * rows] = (
            total[...] + dot(far_grads[side], fars[1 - side]) + dot(relay_grads[side], relays[1 - side])
        )

    @pl.when(rim[0] > 0)
    def _():
        copy = pltpu.make_async_copy(late, spare, spare_sem)
        copy.start()
        copy.wait()
        lates = halves(spare)
        late_grads = side_grads(scale, offset, mine, lates)
        for side in range(2):
            full[side * rows : (side + 1) * rows] += dot(late_grads[side], lates[1 - side])

    copies = []
    for side, out in enumerate((out_x, out_y)):
        loads[side].wait()
        for c in range(CHUNKS):
            part = slice(side * rows + c * step, side * rows + (c + 1) * step)
            wide = raw[part].astype(F32)
            inv = inverse_norm(wide)
            grad = scale[0] * full[part]
            along = inv * inv * jnp.sum(wide * grad, axis=-1, keepdims=True)
            full[part] = (grad - wide * along) * inv
            copy = pltpu.make_async_copy(
                full.at[pl.ds(side * rows + c * step, step)],
                out.at[pl.ds(c * step, step)],
                sem.at[side * CHUNKS + c],
            )
            copy.start()
            copies.append(copy)
    for copy in copies:
        copy.wait()


VMEM = pl.BlockSpec(memory_space=pltpu.VMEM)
SMEM = pl.BlockSpec(memory_space=pltpu.SMEM)
ANY = pl.BlockSpec(memory_space=pl.ANY)


def call(kernel, outs, arrays, small=0, loose=0, in_spec=VMEM, out_spec=VMEM, scratch=()):
    return pl.pallas_call(
        kernel,
        out_shape=[jax.ShapeDtypeStruct(*o) for o in outs],
        in_specs=[SMEM] * small + [in_spec] * (len(arrays) - small - loose) + [ANY] * loose,
        out_specs=[out_spec] * len(outs),
        scratch_shapes=list(scratch),
        compiler_params=pltpu.CompilerParams(vmem_limit_bytes=12 * MIB),
        cost_estimate=pl.CostEstimate(flops=1, bytes_accessed=1, transcendentals=0),
    )(*arrays)


def after(value, *events):
    return lax.optimization_barrier((value, *events))[0]


def per_device(picture_embeds, caption_embeds, sharpness_factor, offset_term):
    scalars = (sharpness_factor, offset_term)
    n = lax.axis_size(AXES)
    rows, width = picture_embeds.shape
    one, two, square = (rows, width), (2 * rows, width), (rows, rows)
    here = lax.axis_index(AXES)
    rim = jnp.where(here == 0, 1, jnp.where(here == n - 1, 2, 0)).astype(jnp.int32).reshape(1)

    near = [(g, (g + 2) % n if g % 2 else (g - 2) % n) for g in range(n)]
    far = [(g, (g - 2) % n if g % 2 else (g + 2) % n) for g in range(n) if g not in (1, n - 2)]
    swap = [(g, g ^ 1) for g in range(n)]
    closing = [(0, n - 1), (n - 2, 0)]

    def sent(value, perm):
        return lax.ppermute(value, AXES, perm)

    near_y = sent(caption_embeds, near)
    near_x = sent(picture_embeds, near)
    (pair,) = call(
        prepare_kernel,
        [(two, BF16)],
        (picture_embeds, caption_embeds),
        in_spec=ANY,
        scratch=[pltpu.VMEM(two, BF16), pltpu.SemaphoreType.DMA((2 * CHUNKS,))],
    )
    far_pair = sent(pair, far)
    mate_pair = sent(pair, swap)
    picked, *grads = call(
        early_kernel, [(two, BF16)] + [(square, BF16)] * 3, (rim, *scalars, pair, mate_pair), small=3
    )
    late_pair = sent(after(picked, near_y), closing)
    relay_y = sent(after(near_y, *grads), swap)
    relay_x = sent(after(near_x, *grads), swap)
    sums = call(
        middle_kernel,
        [(one, F32)] * 2,
        (*scalars, pair, mate_pair, *grads, near_x, near_y),
        small=2,
        loose=2,
        scratch=[pltpu.VMEM(one, BF16), pltpu.VMEM(one, BF16), pltpu.SemaphoreType.DMA((2,))],
    )
    return call(
        end_kernel,
        [(one, F32)] * 2,
        (rim, *scalars, pair, *sums, far_pair, relay_x, relay_y, picture_embeds, caption_embeds, late_pair),
        small=3,
        loose=3,
        out_spec=ANY,
        scratch=[
            pltpu.VMEM(two, F32),
            pltpu.VMEM(two, BF16),
            pltpu.VMEM(two, BF16),
            pltpu.SemaphoreType.DMA((2,)),
            pltpu.SemaphoreType.DMA(()),
            pltpu.SemaphoreType.DMA((2 * CHUNKS,)),
        ],
    )


def solution(mesh):
    return jax.shard_map(
        per_device,
        mesh=mesh,
        in_specs=(P(AXES, None), P(AXES, None), P(), P()),
        out_specs=(P(AXES, None), P(AXES, None)),
        check_vma=False,
    )
```

```python
import jax
import jax.numpy as jnp
from jax import lax
from jax.experimental import pallas as pl
from jax.experimental.pallas import tpu as pltpu
from jax.sharding import PartitionSpec as P

HALF = 2
SPAN = 2 * HALF + 1
AXES = ("outer", "blk")
MIB = 1024 * 1024
CHUNKS = 4
F32, BF16 = jnp.float32, jnp.bfloat16


def inverse_norm(wide):
    return 1.0 / jnp.sqrt(jnp.sum(wide * wide, axis=-1, keepdims=True) + 1e-06)


def normalized(block):
    wide = block.astype(F32)
    return (wide * inverse_norm(wide)).astype(BF16)


def dot(a, b):
    return jnp.dot(a, b, preferred_element_type=F32)


def logits(scale, offset, own_n, other_n):
    z = lax.dot_general(own_n, other_n, (((1,), (1,)), ((), ())), preferred_element_type=F32)
    return scale[0] * z + offset[0]


def pair_grad(scale, offset, own_n, other_n):
    return (jax.nn.sigmoid(logits(scale, offset, own_n, other_n)) / SPAN).astype(BF16)


def halves(ref):
    rows = ref.shape[0] // 2
    return ref[:rows], ref[rows:]


def side_grads(scale, offset, mine, theirs):
    return [pair_grad(scale, offset, own_n, other_n) for own_n, other_n in zip(mine, theirs[::-1])]


def prepare_kernel(x, y, pair, raw, sem):
    rows = x.shape[0]
    step = rows // CHUNKS
    copies = []
    for side, source in enumerate((x, y)):
        for c in range(CHUNKS):
            copies.append(
                pltpu.make_async_copy(
                    source.at[pl.ds(c * step, step)],
                    raw.at[pl.ds(side * rows + c * step, step)],
                    sem.at[side * CHUNKS + c],
                )
            )
    for copy in copies:
        copy.start()
    for c, copy in enumerate(copies):
        copy.wait()
        part = slice(c * step, (c + 1) * step)
        wide = raw[part].astype(F32)
        pair[part] = (wide * inverse_norm(wide)).astype(BF16)


def early_kernel(rim, scale, offset, pair, mate_x, mate_y, picked, mates, own_grad, mate_grad_x, mate_grad_y):
    rows = mate_x.shape[0]
    mates[:rows] = normalized(mate_x[...])
    mates[rows:] = normalized(mate_y[...])

    @pl.when(rim[0] == 1)
    def _():
        picked[...] = mates[...]

    @pl.when(rim[0] != 1)
    def _():
        picked[...] = pair[...]

    mine = halves(pair)
    z = logits(scale, offset, *mine)
    rows = lax.broadcasted_iota(jnp.int32, z.shape, 0)
    cols = lax.broadcasted_iota(jnp.int32, z.shape, 1)
    label = jnp.where(rows == cols, 1.0, -1.0).astype(F32)
    own_grad[...] = (-label * jax.nn.sigmoid(-label * z) / SPAN).astype(BF16)
    mate_grad_x[...], mate_grad_y[...] = side_grads(scale, offset, mine, halves(mates))


def middle_kernel(
    scale, offset, pair, mates, own_grad, mate_grad_x, mate_grad_y, near, sum_x, sum_y, held, sem
):
    copy = pltpu.make_async_copy(near, held, sem)
    copy.start()
    mine = halves(pair)
    mate_x, mate_y = halves(mates)
    sum_x[...] = dot(own_grad[...], mine[1]) + dot(mate_grad_x[...], mate_y)
    sum_y[...] = lax.dot_general(
        own_grad[...], mine[0], (((0,), (0,)), ((), ())), preferred_element_type=F32
    ) + dot(mate_grad_y[...], mate_x)
    copy.wait()
    nears = halves(held)
    grad_x, grad_y = side_grads(scale, offset, mine, nears)
    sum_x[...] += dot(grad_x, nears[1])
    sum_y[...] += dot(grad_y, nears[0])


def end_kernel(
    rim, scale, offset, pair, total_x, total_y, far, relayed, x, y, late,
    out_x, out_y, full, raw, spare, raw_sem, spare_sem, sem,
):
    rows = total_x.shape[0]
    step = rows // CHUNKS
    loads = [
        pltpu.make_async_copy(source, raw.at[pl.ds(side * rows, rows)], raw_sem.at[side])
        for side, source in enumerate((x, y))
    ]
    for load in loads:
        load.start()
    mine, fars = halves(pair), halves(far)
    relays = halves(relayed)
    far_grads = side_grads(scale, offset, mine, fars)
    relay_grads = side_grads(scale, offset, mine, relays)
    for side, total in enumerate((total_x, total_y)):
        full[side * rows : (side + 1) * rows] = (
            total[...] + dot(far_grads[side], fars[1 - side]) + dot(relay_grads[side], relays[1 - side])
        )

    @pl.when(rim[0] > 0)
    def _():
        copy = pltpu.make_async_copy(late, spare, spare_sem)
        copy.start()
        copy.wait()
        lates = halves(spare)
        late_grads = side_grads(scale, offset, mine, lates)
        for side in range(2):
            full[side * rows : (side + 1) * rows] += dot(late_grads[side], lates[1 - side])

    copies = []
    for side, out in enumerate((out_x, out_y)):
        loads[side].wait()
        for c in range(CHUNKS):
            part = slice(side * rows + c * step, side * rows + (c + 1) * step)
            wide = raw[part].astype(F32)
            inv = inverse_norm(wide)
            grad = scale[0] * full[part]
            along = inv * inv * jnp.sum(wide * grad, axis=-1, keepdims=True)
            full[part] = (grad - wide * along) * inv
            copy = pltpu.make_async_copy(
                full.at[pl.ds(side * rows + c * step, step)],
                out.at[pl.ds(c * step, step)],
                sem.at[side * CHUNKS + c],
            )
            copy.start()
            copies.append(copy)
    for copy in copies:
        copy.wait()


VMEM = pl.BlockSpec(memory_space=pltpu.VMEM)
SMEM = pl.BlockSpec(memory_space=pltpu.SMEM)
ANY = pl.BlockSpec(memory_space=pl.ANY)


def call(kernel, outs, arrays, small=0, loose=0, in_spec=VMEM, out_spec=VMEM, scratch=()):
    return pl.pallas_call(
        kernel,
        out_shape=[jax.ShapeDtypeStruct(*o) for o in outs],
        in_specs=[SMEM] * small + [in_spec] * (len(arrays) - small - loose) + [ANY] * loose,
        out_specs=[out_spec] * len(outs),
        scratch_shapes=list(scratch),
        compiler_params=pltpu.CompilerParams(vmem_limit_bytes=12 * MIB),
        cost_estimate=pl.CostEstimate(flops=1, bytes_accessed=1, transcendentals=0),
    )(*arrays)


def after(value, *events):
    return lax.optimization_barrier((value, *events))[0]


def per_device(picture_embeds, caption_embeds, sharpness_factor, offset_term):
    scalars = (sharpness_factor, offset_term)
    n = lax.axis_size(AXES)
    rows, width = picture_embeds.shape
    one, two, square = (rows, width), (2 * rows, width), (rows, rows)
    here = lax.axis_index(AXES)
    rim = jnp.where(here == 0, 1, jnp.where(here == n - 1, 2, 0)).astype(jnp.int32).reshape(1)

    near = [(g, (g + 2) % n if g % 2 else (g - 2) % n) for g in range(n)]
    far = [(g, (g - 2) % n if g % 2 else (g + 2) % n) for g in range(n) if g not in (1, n - 2)]
    swap = [(g, g ^ 1) for g in range(n)]
    closing = [(0, n - 1), (n - 2, 0)]

    def sent(value, perm):
        return lax.ppermute(value, AXES, perm)

    mate_y = sent(caption_embeds, swap)
    (pair,) = call(
        prepare_kernel,
        [(two, BF16)],
        (picture_embeds, caption_embeds),
        in_spec=ANY,
        scratch=[pltpu.VMEM(two, BF16), pltpu.SemaphoreType.DMA((2 * CHUNKS,))],
    )
    near_pair = sent(pair, near)
    far_pair = sent(pair, far)
    mate_x = sent(picture_embeds, swap)
    picked, *mate_terms = call(
        early_kernel, [(two, BF16)] * 2 + [(square, BF16)] * 3, (rim, *scalars, pair, mate_x, mate_y), small=3
    )
    late_pair = sent(picked, closing)
    relayed_pair = sent(near_pair, swap)
    sums = call(
        middle_kernel,
        [(one, F32)] * 2,
        (*scalars, pair, *mate_terms, near_pair),
        small=2,
        loose=1,
        scratch=[pltpu.VMEM(two, BF16), pltpu.SemaphoreType.DMA(())],
    )
    return call(
        end_kernel,
        [(one, F32)] * 2,
        (rim, *scalars, pair, *sums, far_pair, relayed_pair, picture_embeds, caption_embeds, late_pair),
        small=3,
        loose=3,
        out_spec=ANY,
        scratch=[
            pltpu.VMEM(two, F32),
            pltpu.VMEM(two, BF16),
            pltpu.VMEM(two, BF16),
            pltpu.SemaphoreType.DMA((2,)),
            pltpu.SemaphoreType.DMA(()),
            pltpu.SemaphoreType.DMA((2 * CHUNKS,)),
        ],
    )


def solution(mesh):
    return jax.shard_map(
        per_device,
        mesh=mesh,
        in_specs=(P(AXES, None), P(AXES, None), P(), P()),
        out_specs=(P(AXES, None), P(AXES, None)),
        check_vma=False,
    )
```

```python
import jax
import jax.numpy as jnp
from jax import lax
from jax.experimental import pallas as pl
from jax.experimental.pallas import tpu as pltpu
from jax.sharding import PartitionSpec as P

HALF = 2
SPAN = 2 * HALF + 1
AXES = ("outer", "blk")
MIB = 1024 * 1024
CHUNKS = 4
F32, BF16 = jnp.float32, jnp.bfloat16


def inverse_norm(wide):
    return 1.0 / jnp.sqrt(jnp.sum(wide * wide, axis=-1, keepdims=True) + 1e-06)


def normalized(block):
    wide = block.astype(F32)
    return (wide * inverse_norm(wide)).astype(BF16)


def dot(a, b):
    return jnp.dot(a, b, preferred_element_type=F32)


def logits(scale, offset, own_n, other_n):
    z = lax.dot_general(own_n, other_n, (((1,), (1,)), ((), ())), preferred_element_type=F32)
    return scale[0] * z + offset[0]


def pair_grad(scale, offset, own_n, other_n):
    return (jax.nn.sigmoid(logits(scale, offset, own_n, other_n)) / SPAN).astype(BF16)


def halves(ref):
    rows = ref.shape[0] // 2
    return ref[:rows], ref[rows:]


def side_grads(scale, offset, mine, theirs):
    return [pair_grad(scale, offset, own_n, other_n) for own_n, other_n in zip(mine, theirs[::-1])]


def prepare_kernel(x, y, pair, raw, sem):
    rows = x.shape[0]
    step = rows // CHUNKS
    copies = []
    for side, source in enumerate((x, y)):
        for c in range(CHUNKS):
            copies.append(
                pltpu.make_async_copy(
                    source.at[pl.ds(c * step, step)],
                    raw.at[pl.ds(side * rows + c * step, step)],
                    sem.at[side * CHUNKS + c],
                )
            )
    for copy in copies:
        copy.start()
    for c, copy in enumerate(copies):
        copy.wait()
        part = slice(c * step, (c + 1) * step)
        wide = raw[part].astype(F32)
        pair[part] = (wide * inverse_norm(wide)).astype(BF16)


def pick_kernel(rim, pair, mate_x, mate_y, picked, held, sem):
    rows = mate_x.shape[0]

    @pl.when(rim[0] == 1)
    def _():
        copies = [
            pltpu.make_async_copy(source, held.at[pl.ds(side * rows, rows)], sem.at[side])
            for side, source in enumerate((mate_x, mate_y))
        ]
        for copy in copies:
            copy.start()
        for copy in copies:
            copy.wait()
        picked[...] = normalized(held[...])

    @pl.when(rim[0] != 1)
    def _():
        picked[...] = pair[...]


def early_kernel(scale, offset, pair, mate_x, mate_y, mates, own_grad, mate_grad_x, mate_grad_y):
    rows = mate_x.shape[0]
    mates[:rows] = normalized(mate_x[...])
    mates[rows:] = normalized(mate_y[...])
    mine = halves(pair)
    z = logits(scale, offset, *mine)
    rows = lax.broadcasted_iota(jnp.int32, z.shape, 0)
    cols = lax.broadcasted_iota(jnp.int32, z.shape, 1)
    label = jnp.where(rows == cols, 1.0, -1.0).astype(F32)
    own_grad[...] = (-label * jax.nn.sigmoid(-label * z) / SPAN).astype(BF16)
    mate_grad_x[...], mate_grad_y[...] = side_grads(scale, offset, mine, halves(mates))


def middle_kernel(
    rim, scale, offset, pair, mates, own_grad, mate_grad_x, mate_grad_y, near, first_far, sum_x, sum_y,
    held, spare, sem,
):
    near_copy = pltpu.make_async_copy(near, held, sem.at[0])
    near_copy.start()
    first_copy = pltpu.make_async_copy(first_far, spare, sem.at[1])

    @pl.when(rim[0] == 3)
    def _():
        first_copy.start()

    mine = halves(pair)
    mate_x, mate_y = halves(mates)
    sum_x[...] = dot(own_grad[...], mine[1]) + dot(mate_grad_x[...], mate_y)
    sum_y[...] = lax.dot_general(
        own_grad[...], mine[0], (((0,), (0,)), ((), ())), preferred_element_type=F32
    ) + dot(mate_grad_y[...], mate_x)
    near_copy.wait()
    nears = halves(held)
    grad_x, grad_y = side_grads(scale, offset, mine, nears)
    sum_x[...] += dot(grad_x, nears[1])
    sum_y[...] += dot(grad_y, nears[0])

    @pl.when(rim[0] == 3)
    def _():
        first_copy.wait()
        firsts = halves(spare)
        first_grads = side_grads(scale, offset, mine, firsts)
        sum_x[...] += dot(first_grads[0], firsts[1])
        sum_y[...] += dot(first_grads[1], firsts[0])


def end_kernel(
    rim, scale, offset, pair, total_x, total_y, far, relayed, x, y, late,
    out_x, out_y, full, raw, spare, raw_sem, spare_sem, sem,
):
    rows = total_x.shape[0]
    step = rows // CHUNKS
    loads = [
        pltpu.make_async_copy(source, raw.at[pl.ds(side * rows, rows)], raw_sem.at[side])
        for side, source in enumerate((x, y))
    ]
    for load in loads:
        load.start()
    mine, fars = halves(pair), halves(far)
    relays = halves(relayed)
    far_grads = side_grads(scale, offset, mine, fars)
    relay_grads = side_grads(scale, offset, mine, relays)
    for side, total in enumerate((total_x, total_y)):
        full[side * rows : (side + 1) * rows] = (
            total[...] + dot(far_grads[side], fars[1 - side]) + dot(relay_grads[side], relays[1 - side])
        )

    @pl.when((rim[0] == 1) | (rim[0] == 2))
    def _():
        copy = pltpu.make_async_copy(late, spare, spare_sem)
        copy.start()
        copy.wait()
        lates = halves(spare)
        late_grads = side_grads(scale, offset, mine, lates)
        for side in range(2):
            full[side * rows : (side + 1) * rows] += dot(late_grads[side], lates[1 - side])

    copies = []
    for side, out in enumerate((out_x, out_y)):
        loads[side].wait()
        for c in range(CHUNKS):
            part = slice(side * rows + c * step, side * rows + (c + 1) * step)
            wide = raw[part].astype(F32)
            inv = inverse_norm(wide)
            grad = scale[0] * full[part]
            along = inv * inv * jnp.sum(wide * grad, axis=-1, keepdims=True)
            full[part] = (grad - wide * along) * inv
            copy = pltpu.make_async_copy(
                full.at[pl.ds(side * rows + c * step, step)],
                out.at[pl.ds(c * step, step)],
                sem.at[side * CHUNKS + c],
            )
            copy.start()
            copies.append(copy)
    for copy in copies:
        copy.wait()


VMEM = pl.BlockSpec(memory_space=pltpu.VMEM)
SMEM = pl.BlockSpec(memory_space=pltpu.SMEM)
ANY = pl.BlockSpec(memory_space=pl.ANY)


def call(kernel, outs, arrays, small=0, loose=0, in_spec=VMEM, out_spec=VMEM, scratch=()):
    return pl.pallas_call(
        kernel,
        out_shape=[jax.ShapeDtypeStruct(*o) for o in outs],
        in_specs=[SMEM] * small + [in_spec] * (len(arrays) - small - loose) + [ANY] * loose,
        out_specs=[out_spec] * len(outs),
        scratch_shapes=list(scratch),
        compiler_params=pltpu.CompilerParams(vmem_limit_bytes=12 * MIB),
        cost_estimate=pl.CostEstimate(flops=1, bytes_accessed=1, transcendentals=0),
    )(*arrays)


def after(value, *events):
    return lax.optimization_barrier((value, *events))[0]


def per_device(picture_embeds, caption_embeds, sharpness_factor, offset_term):
    scalars = (sharpness_factor, offset_term)
    n = lax.axis_size(AXES)
    rows, width = picture_embeds.shape
    one, two, square = (rows, width), (2 * rows, width), (rows, rows)
    here = lax.axis_index(AXES)
    rim = jnp.where(here == 0, 1, jnp.where(here == n - 1, 2, jnp.where(here == 1, 3, 0))).astype(jnp.int32).reshape(1)

    near = [(g, (g + 2) % n if g % 2 else (g - 2) % n) for g in range(n)]
    far = [(g, (g - 2) % n if g % 2 else (g + 2) % n) for g in range(n) if g not in (1, 3, n - 2)]
    swap = [(g, g ^ 1) for g in range(n)]
    closing = [(0, n - 1), (n - 2, 0)]

    def sent(value, perm):
        return lax.ppermute(value, AXES, perm)

    mate_y = sent(caption_embeds, swap)
    (pair,) = call(
        prepare_kernel,
        [(two, BF16)],
        (picture_embeds, caption_embeds),
        in_spec=ANY,
        scratch=[pltpu.VMEM(two, BF16), pltpu.SemaphoreType.DMA((2 * CHUNKS,))],
    )
    near_pair = sent(pair, near)
    far_pair = sent(pair, far)
    first_far = sent(pair, [(3, 1)])
    mate_x = sent(picture_embeds, swap)
    (picked,) = call(
        pick_kernel,
        [(two, BF16)],
        (rim, pair, mate_x, mate_y),
        small=1,
        loose=2,
        scratch=[pltpu.VMEM(two, BF16), pltpu.SemaphoreType.DMA((2,))],
    )
    late_pair = sent(after(picked, first_far), closing)
    mate_terms = call(
        early_kernel, [(two, BF16)] + [(square, BF16)] * 3, (*scalars, pair, mate_x, mate_y), small=2
    )
    relayed_pair = sent(after(near_pair, *mate_terms), swap)
    sums = call(
        middle_kernel,
        [(one, F32)] * 2,
        (rim, *scalars, pair, *mate_terms, near_pair, first_far),
        small=3,
        loose=2,
        scratch=[pltpu.VMEM(two, BF16), pltpu.VMEM(two, BF16), pltpu.SemaphoreType.DMA((2,))],
    )
    return call(
        end_kernel,
        [(one, F32)] * 2,
        (rim, *scalars, pair, *sums, far_pair, relayed_pair, picture_embeds, caption_embeds, late_pair),
        small=3,
        loose=3,
        out_spec=ANY,
        scratch=[
            pltpu.VMEM(two, F32),
            pltpu.VMEM(two, BF16),
            pltpu.VMEM(two, BF16),
            pltpu.SemaphoreType.DMA((2,)),
            pltpu.SemaphoreType.DMA(()),
            pltpu.SemaphoreType.DMA((2 * CHUNKS,)),
        ],
    )


def solution(mesh):
    return jax.shard_map(
        per_device,
        mesh=mesh,
        in_specs=(P(AXES, None), P(AXES, None), P(), P()),
        out_specs=(P(AXES, None), P(AXES, None)),
        check_vma=False,
    )
```

```python
import jax
import jax.numpy as jnp
from jax import lax
from jax.experimental import pallas as pl
from jax.experimental.pallas import tpu as pltpu
from jax.sharding import PartitionSpec as P

HALF = 2
SPAN = 2 * HALF + 1
AXES = ("outer", "blk")
MIB = 1024 * 1024
CHUNKS = 8
COLUMNS = 256
F32, BF16 = jnp.float32, jnp.bfloat16


def inverse_norm(wide):
    return 1.0 / jnp.sqrt(jnp.sum(wide * wide, axis=-1, keepdims=True) + 1e-06)


def normalized(block):
    wide = block.astype(F32)
    return (wide * inverse_norm(wide)).astype(BF16)


def dot(a, b):
    return jnp.dot(a, b, preferred_element_type=F32)


def accumulate(out, at, base, terms):
    for start in range(0, out.shape[1], COLUMNS):
        cols = slice(start, min(start + COLUMNS, out.shape[1]))
        total = None if base is None else base[:, cols]
        for a, b in terms:
            part = dot(a, b[:, cols])
            total = part if total is None else total + part
        out[at, cols] = total


def logits(scale, offset, own_n, other_n):
    z = lax.dot_general(own_n, other_n, (((1,), (1,)), ((), ())), preferred_element_type=F32)
    return scale[0] * z + offset[0]


def pair_grad(scale, offset, own_n, other_n):
    return (jax.nn.sigmoid(logits(scale, offset, own_n, other_n)) / SPAN).astype(BF16)


def halves(ref):
    rows = ref.shape[0] // 2
    return ref[:rows], ref[rows:]


def side_grads(scale, offset, mine, theirs):
    return [pair_grad(scale, offset, own_n, other_n) for own_n, other_n in zip(mine, theirs[::-1])]


def prepare_kernel(x, y, pair, raw, sem):
    rows = x.shape[0]
    step = rows // CHUNKS
    copies = []
    for side, source in enumerate((x, y)):
        for c in range(CHUNKS):
            copies.append(
                pltpu.make_async_copy(
                    source.at[pl.ds(c * step, step)],
                    raw.at[pl.ds(side * rows + c * step, step)],
                    sem.at[side * CHUNKS + c],
                )
            )
    for copy in copies:
        copy.start()
    for c, copy in enumerate(copies):
        copy.wait()
        part = slice(c * step, (c + 1) * step)
        wide = raw[part].astype(F32)
        pair[part] = (wide * inverse_norm(wide)).astype(BF16)


def early_kernel(rim, scale, offset, pair, mate_x, mate_y, picked, mates, own_grad, mate_grad_x, mate_grad_y):
    rows = mate_x.shape[0]
    mates[:rows] = normalized(mate_x[...])
    mates[rows:] = normalized(mate_y[...])

    @pl.when(rim[0] == 1)
    def _():
        picked[...] = mates[...]

    @pl.when(rim[0] != 1)
    def _():
        picked[...] = pair[...]

    mine = halves(pair)
    z = logits(scale, offset, *mine)
    rows = lax.broadcasted_iota(jnp.int32, z.shape, 0)
    cols = lax.broadcasted_iota(jnp.int32, z.shape, 1)
    label = jnp.where(rows == cols, 1.0, -1.0).astype(F32)
    own_grad[...] = (-label * jax.nn.sigmoid(-label * z) / SPAN).astype(BF16)
    mate_grad_x[...], mate_grad_y[...] = side_grads(scale, offset, mine, halves(mates))


def middle_kernel(scale, offset, pair, mates, own_grad, mate_grad_x, mate_grad_y, near, sum_x, sum_y):
    mine, nears = halves(pair), halves(near)
    mate_x, mate_y = halves(mates)
    grad_x, grad_y = side_grads(scale, offset, mine, nears)
    accumulate(
        sum_x, slice(None), None, [(own_grad[...], mine[1]), (mate_grad_x[...], mate_y), (grad_x, nears[1])]
    )
    accumulate(
        sum_y, slice(None), None, [(own_grad[...].T, mine[0]), (mate_grad_y[...], mate_x), (grad_y, nears[0])]
    )


def end_kernel(
    rim, scale, offset, pair, total_x, total_y, far, relayed, x, y, late,
    out_x, out_y, full, raw, spare, raw_sem, spare_sem, sem,
):
    rows = total_x.shape[0]
    step = rows // CHUNKS
    loads = [
        pltpu.make_async_copy(source, raw.at[pl.ds(side * rows, rows)], raw_sem.at[side])
        for side, source in enumerate((x, y))
    ]
    for load in loads:
        load.start()
    mine, fars = halves(pair), halves(far)
    relays = halves(relayed)
    far_grads = side_grads(scale, offset, mine, fars)
    relay_grads = side_grads(scale, offset, mine, relays)
    for side, total in enumerate((total_x, total_y)):
        accumulate(
            full,
            slice(side * rows, (side + 1) * rows),
            total,
            [(far_grads[side], fars[1 - side]), (relay_grads[side], relays[1 - side])],
        )

    @pl.when(rim[0] > 0)
    def _():
        copy = pltpu.make_async_copy(late, spare, spare_sem)
        copy.start()
        copy.wait()
        lates = halves(spare)
        late_grads = side_grads(scale, offset, mine, lates)
        for side in range(2):
            full[side * rows : (side + 1) * rows] += dot(late_grads[side], lates[1 - side])

    copies = []
    for side, out in enumerate((out_x, out_y)):
        loads[side].wait()
        for c in range(CHUNKS):
            part = slice(side * rows + c * step, side * rows + (c + 1) * step)
            wide = raw[part].astype(F32)
            inv = inverse_norm(wide)
            grad = scale[0] * full[part]
            along = inv * inv * jnp.sum(wide * grad, axis=-1, keepdims=True)
            full[part] = (grad - wide * along) * inv
            copy = pltpu.make_async_copy(
                full.at[pl.ds(side * rows + c * step, step)],
                out.at[pl.ds(c * step, step)],
                sem.at[side * CHUNKS + c],
            )
            copy.start()
            copies.append(copy)
    for copy in copies:
        copy.wait()


VMEM = pl.BlockSpec(memory_space=pltpu.VMEM)
SMEM = pl.BlockSpec(memory_space=pltpu.SMEM)
ANY = pl.BlockSpec(memory_space=pl.ANY)


def call(kernel, outs, arrays, small=0, loose=0, in_spec=VMEM, out_spec=VMEM, scratch=()):
    return pl.pallas_call(
        kernel,
        out_shape=[jax.ShapeDtypeStruct(*o) for o in outs],
        in_specs=[SMEM] * small + [in_spec] * (len(arrays) - small - loose) + [ANY] * loose,
        out_specs=[out_spec] * len(outs),
        scratch_shapes=list(scratch),
        compiler_params=pltpu.CompilerParams(vmem_limit_bytes=12 * MIB),
        cost_estimate=pl.CostEstimate(flops=1, bytes_accessed=1, transcendentals=0),
    )(*arrays)


def after(value, *events):
    return lax.optimization_barrier((value, *events))[0]


def per_device(picture_embeds, caption_embeds, sharpness_factor, offset_term):
    scalars = (sharpness_factor, offset_term)
    n = lax.axis_size(AXES)
    rows, width = picture_embeds.shape
    one, two, square = (rows, width), (2 * rows, width), (rows, rows)
    here = lax.axis_index(AXES)
    rim = jnp.where(here == 0, 1, jnp.where(here == n - 1, 2, 0)).astype(jnp.int32).reshape(1)

    near = [(g, (g + 2) % n if g % 2 else (g - 2) % n) for g in range(n)]
    far = [(g, (g - 2) % n if g % 2 else (g + 2) % n) for g in range(n) if g not in (1, n - 2)]
    swap = [(g, g ^ 1) for g in range(n)]
    closing = [(0, n - 1), (n - 2, 0)]

    def sent(value, perm):
        return lax.ppermute(value, AXES, perm)

    mate_y = sent(caption_embeds, swap)
    (pair,) = call(
        prepare_kernel,
        [(two, BF16)],
        (picture_embeds, caption_embeds),
        in_spec=ANY,
        scratch=[pltpu.VMEM(two, BF16), pltpu.SemaphoreType.DMA((2 * CHUNKS,))],
    )
    near_pair = sent(pair, near)
    far_pair = sent(pair, far)
    mate_x = sent(picture_embeds, swap)
    picked, *mate_terms = call(
        early_kernel, [(two, BF16)] * 2 + [(square, BF16)] * 3, (rim, *scalars, pair, mate_x, mate_y), small=3
    )
    late_pair = sent(picked, closing)
    relayed_pair = sent(near_pair, swap)
    sums = call(
        middle_kernel,
        [(one, F32)] * 2,
        (*scalars, pair, *mate_terms, near_pair),
        small=2,
    )
    return call(
        end_kernel,
        [(one, F32)] * 2,
        (rim, *scalars, pair, *sums, far_pair, relayed_pair, picture_embeds, caption_embeds, late_pair),
        small=3,
        loose=3,
        out_spec=ANY,
        scratch=[
            pltpu.VMEM(two, F32),
            pltpu.VMEM(two, BF16),
            pltpu.VMEM(two, BF16),
            pltpu.SemaphoreType.DMA((2,)),
            pltpu.SemaphoreType.DMA(()),
            pltpu.SemaphoreType.DMA((2 * CHUNKS,)),
        ],
    )


def solution(mesh):
    return jax.shard_map(
        per_device,
        mesh=mesh,
        in_specs=(P(AXES, None), P(AXES, None), P(), P()),
        out_specs=(P(AXES, None), P(AXES, None)),
        check_vma=False,
    )
```
